512 devices in a mesh: frame: 32 (over z_hi, y, x), tensor: 16 (over z_lo, core).
Axes of the slice: x: 4, y: 4, z: 16 (z_hi: 2, z_lo: 8; z = z_hi * 8 + z_lo), core: 2. Of those that a mesh axis runs over, the one named last changes fastest.
Arguments:
- tokens: bfloat16 [16384, 1, 4096], P(('frame', 'tensor')), may hold values from -6 to 6
- norm_gain: float32 [4096], replicated, may hold values from 0.5 to 1.5
- query_weight: bfloat16 [4096, 4096], P(None, 'tensor'), may hold values from -0.09375 to 0.09375
- out_weight: bfloat16 [4096, 4096], P('tensor'), may hold values from -0.09375 to 0.09375
- cache_keys: bfloat16 [1536, 1, 4096], P('frame', None, 'tensor'), may hold values from -420 to 420
- cache_values: bfloat16 [1536, 1, 4096], P('frame', None, 'tensor'), may hold values from -18 to 18
- token_pos: int32 [16384, 1], P('frame'), may hold values from 0 to 1535, as said below
- frame_pad: int32 [1], replicated, may hold values from 0 to 768
Outputs:
- mixed: bfloat16 [16384, 1, 4096], P(('frame', 'tensor'))
The draws below stay inside these ranges and needn't reach their ends.
Inputs may be any that keep to these rules, and one draw needn't show every extreme that they name: `token_pos`: nondecreasing along each sequence; the last token of every sequence has 1535.
All inputs are finite; a program needn't handle non-finite values.
Results may differ from the reference program's by a relative error of at most 0.018.
Values may be sent and summed in bfloat16 or wider, within the bound.
No kernel may reach another device: no remote copies, remote signals or barrier semaphores. Data moves between devices by JAX's collectives and lax.ppermute only.
A program may use at most 64 MiB of HBM per device.

```python
import jax
import jax.numpy as jnp
from jax import lax

D = 4096
HEADS = 32
HEAD_DIM = 128
SEQS = 1
LENGTH = 16384
FRAMES = 1536
N_TENSOR = 16


def draw_token_pos(key, part):
    climbs = jax.random.randint(jax.random.fold_in(key, 11), (LENGTH, SEQS), 0, 3)
    climbed = jnp.cumsum(climbs, axis=0)
    placed = jnp.minimum(climbed * FRAMES // LENGTH, FRAMES - 1)
    finals = jnp.arange(LENGTH)[:, None] == LENGTH - 1
    return jnp.where(finals, FRAMES - 1, placed).astype(jnp.int32)


def draw_cache_keys(key, part):
    shape = (FRAMES, SEQS, HEADS * HEAD_DIM)
    base = 2.0 * jax.random.normal(jax.random.fold_in(key, 23), shape, jnp.float32)
    return jnp.clip(base, -12.0, 12.0).astype(jnp.bfloat16)


def block_scale(stream_key, extent, shards, smallest, top_value):
    level, own = 1.0, jax.random.fold_in(stream_key, 6)
    for dim, blocks in shards:
        draws = jnp.exp(jax.random.uniform(jax.random.fold_in(own, dim), (blocks,), jnp.float32, smallest / len(shards), top_value / len(shards)))
        level = level * jnp.repeat(draws, extent[dim] // blocks).reshape([-1 if axis == dim else 1 for axis in range(len(extent))])
    return level


def bell_draw(key, dims, spread, bound, split=(), kind=jnp.bfloat16):
    drawn = spread * jax.random.normal(key, dims, jnp.float32)
    if split:
        drawn = drawn * block_scale(key, dims, split, -0.22, 0.18)
    return jnp.clip(drawn, -bound, bound).astype(kind)


def setup_inputs(seed: int = 0) -> dict:
    keys = jax.random.split(jax.random.key(seed), 9)
    tokens = bell_draw(keys[0], (LENGTH, SEQS, D), 1.0, 6.0, ((0, 512),))
    norm_gain = jnp.clip(1.0 + 0.1 * jax.random.normal(keys[1], (D,), jnp.float32), 0.5, 1.5)
    query_weight = bell_draw(keys[2], (D, HEADS * HEAD_DIM), D ** -0.5, 0.09375, ((1, 16),))
    out_weight = bell_draw(keys[3], (HEADS * HEAD_DIM, D), (HEADS * HEAD_DIM) ** -0.5, 0.09375, ((0, 16),))
    cache_keys = draw_cache_keys(jax.random.fold_in(keys[8], 71), 0)
    cache_values = bell_draw(keys[5], (FRAMES, SEQS, HEADS * HEAD_DIM), 3.0, 18.0, ((0, 32), (2, 16)))
    token_pos = draw_token_pos(jax.random.fold_in(keys[8], 71), 0)
    frame_pad = jax.random.randint(keys[7], (SEQS,), 0, FRAMES // 2 + 1).astype(jnp.int32)
    return {"tokens": tokens, "norm_gain": norm_gain, "query_weight": query_weight, "out_weight": out_weight, "cache_keys": cache_keys, "cache_values": cache_values, "token_pos": token_pos, "frame_pad": frame_pad}


epsilon = 1e-06
masked_score = -1e+30

def reference(tokens, norm_gain, query_weight, out_weight, cache_keys, cache_values, token_pos, frame_pad):
    hidden = tokens.astype(jnp.float32)
    factor = lax.rsqrt(lax.optimization_barrier(jnp.mean(hidden * hidden, axis=-1, keepdims=True)) + epsilon)
    normed = (hidden * factor * norm_gain.astype(jnp.float32)).astype(jnp.bfloat16)
    queries = (jnp.dot(normed, query_weight, preferred_element_type=jnp.float32) * HEAD_DIM ** (-0.5)).astype(jnp.bfloat16)
    frame_index = jnp.arange(FRAMES, dtype=jnp.int32)
    valid_frames = (FRAMES - frame_pad).astype(jnp.int32)
    visible = (frame_index[None, :, None] <= token_pos[:, None, :]) & (frame_index[None, :, None] < valid_frames[None, None, :])
    query_heads = queries.reshape(LENGTH, SEQS, HEADS, HEAD_DIM).transpose(2, 0, 1, 3)
    key_heads = cache_keys.reshape(FRAMES, SEQS, HEADS, HEAD_DIM).transpose(2, 0, 1, 3)
    value_heads = cache_values.reshape(FRAMES, SEQS, HEADS, HEAD_DIM).transpose(2, 0, 1, 3)

    def one_head(operands):
        query_one, key_one, value_one = operands
        scores = jnp.einsum('lsd,fsd->lfs', query_one.astype(jnp.float32), key_one.astype(jnp.float32))
        scores = jnp.where(visible, scores, masked_score)
        highest = lax.optimization_barrier(jnp.max(scores, axis=1, keepdims=True))
        weights = jnp.where(visible, jnp.exp(scores - highest), 0.0)
        summed = lax.optimization_barrier(jnp.sum(weights, axis=1))
        rounded = lax.optimization_barrier(weights.astype(jnp.bfloat16)).astype(jnp.float32)
        gathered = jnp.einsum('lfs,fsd->lsd', rounded, value_one.astype(jnp.float32))
        return (gathered / summed[:, :, None]).astype(jnp.bfloat16)
    attended = lax.map(one_head, (query_heads, key_heads, value_heads))
    per_group = HEADS // N_TENSOR
    groups = attended.reshape(N_TENSOR, per_group, LENGTH, SEQS, HEAD_DIM).transpose(0, 2, 3, 1, 4)
    groups = groups.reshape(N_TENSOR, LENGTH, SEQS, per_group * HEAD_DIM)
    weight_groups = out_weight.reshape(N_TENSOR, per_group * HEAD_DIM, D)

    def add_group(running, operands):
        head_group, weight_group = operands
        partial_value = jnp.dot(head_group, weight_group, preferred_element_type=jnp.float32)
        partial_value = lax.optimization_barrier(partial_value.astype(jnp.bfloat16)).astype(jnp.float32)
        return (running + partial_value, None)
    summed_out, _ = lax.scan(add_group, jnp.zeros((LENGTH, SEQS, D), jnp.float32), (groups, weight_groups))
    return summed_out.astype(jnp.bfloat16)
```

```python
import jax
import jax.numpy as jnp
from jax import lax
from jax.sharding import Mesh, PartitionSpec as P

HEAD_DIM = 128
EPSILON = 1e-06
MASKED = -1e30
RING = ("zh", "zl")
SWAP = [(0, 1), (1, 0)]


def shift(step):
    return [(i, (i + step) % 16) for i in range(16)]


def opposite(step):
    return [
        (2 * i + c, 2 * ((i + (step if c == 0 else -step)) % 16) + c)
        for i in range(16)
        for c in range(2)
    ]


def normalize(rows, gain):
    hidden = rows.astype(jnp.float32)
    factor = lax.rsqrt(jnp.mean(hidden * hidden, axis=-1, keepdims=True) + EPSILON)
    return (hidden * factor * gain).astype(jnp.bfloat16)


def up(x):
    return lax.ppermute(x, RING, shift(1))


def down(x):
    return lax.ppermute(x, RING, shift(-1))


def per_device(tokens, gain, wq, wo, keys, values, token_pos, frame_pad):
    rows = tokens.shape[0]
    zh, zl, core = (lax.axis_index(a) for a in ("zh", "zl", "c"))
    z = zh * 8 + zl

    pos = token_pos.reshape(2, 256)
    mine = jnp.concatenate(
        [
            keys.reshape(48, 256),
            values.reshape(48, 256),
            (pos // 8).astype(jnp.bfloat16),
            (pos % 8).astype(jnp.bfloat16),
            jnp.zeros((4, 256), jnp.bfloat16),
        ]
    )
    theirs = lax.ppermute(mine, "zh", SWAP)
    other_pos = (
        theirs[96:98].astype(jnp.int32) * 8 + theirs[98:100].astype(jnp.int32)
    ).reshape(512)
    kv = jnp.stack([mine[:96], theirs[:96]]).reshape(2, 2, 48, 256)
    kv = lax.all_gather(kv, "x", axis=0)
    k_own = lax.all_gather(kv[:, :, 0], "y", axis=0).reshape(1536, 256)
    v_own = lax.all_gather(kv[:, :, 1], "y", axis=0).reshape(1536, 256)
    k_oth = lax.ppermute(k_own, "c", SWAP)
    v_oth = lax.ppermute(v_own, "c", SWAP)
    index = jnp.arange(1536, dtype=jnp.int32)
    half = (index // 48) % 2
    half = jnp.where(half == 0, zh, 1 - zh)
    frame = (half * 16 + index // 96) * 48 + index % 48

    wq_oth = lax.ppermute(wq, "c", SWAP)
    wo_oth = lax.ppermute(wo, "c", SWAP)

    own = normalize(tokens.reshape(rows, -1), gain)
    p1, m1 = up(own), down(own)
    p2, m2 = up(p1), down(m1)
    p3, m3 = up(p2), down(m2)
    far = lax.ppermute(jnp.where(core == 0, p3, m3), RING + ("c",), opposite(1))
    blocks = [far, p3, m3, p2, m2, p1, m1, own]
    x = jnp.concatenate(blocks)
    sign = jnp.where(core == 0, -4, 4)

    both = jnp.where(zh == 0, jnp.stack([token_pos[:, 0], other_pos]), jnp.stack([other_pos, token_pos[:, 0]])).reshape(16, 2, rows)
    at = jnp.stack([(z + d) % 16 for d in (sign, -3, 3, -2, 2, -1, 1, 0)])
    where = jnp.concatenate([lax.dynamic_slice(both, (at[i], core, 0), (1, 1, rows)).reshape(rows) for i in range(8)])

    visible = (frame[None, :] <= where[:, None]) & (frame[None, :] < 1536 - frame_pad[0])
    outs = []
    for w, k, v in ((wq, k_own, v_own), (wq_oth, k_oth, v_oth)):
        q = (jnp.dot(x, w, preferred_element_type=jnp.float32) * HEAD_DIM**-0.5).astype(jnp.bfloat16)
        q = q.reshape(-1, 2, HEAD_DIM)
        k = k.reshape(-1, 2, HEAD_DIM)
        v = v.reshape(-1, 2, HEAD_DIM)
        s = jnp.einsum("rhd,fhd->rhf", q, k, preferred_element_type=jnp.float32)
        s = jnp.where(visible[:, None, :], s, MASKED)
        top = jnp.max(s, axis=-1, keepdims=True)
        e = jnp.where(visible[:, None, :], jnp.exp(s - top), 0.0)
        total = jnp.sum(e, axis=-1)
        a = jnp.einsum("rhf,fhd->rhd", e.astype(jnp.bfloat16), v, preferred_element_type=jnp.float32)
        outs.append((a / total[..., None]).astype(jnp.bfloat16).reshape(-1, 256))
    part = jnp.dot(outs[0], wo, preferred_element_type=jnp.float32) + jnp.dot(
        outs[1], wo_oth, preferred_element_type=jnp.float32
    )
    rfar, r3p, r3m, r2p, r2m, r1p, r1m, mine_out = jnp.split(part, 8)
    bf = lambda v: v.astype(jnp.bfloat16)
    back = lax.ppermute(bf(rfar), RING + ("c",), opposite(-1)).astype(jnp.float32)
    zero = jnp.zeros_like(back)
    ap = down(bf(r3p + jnp.where(core == 0, back, zero)))
    am = up(bf(r3m + jnp.where(core == 0, zero, back)))
    ap, am = down(bf(r2p + ap)), up(bf(r2m + am))
    ap, am = down(bf(r1p + ap)), up(bf(r1m + am))
    out = mine_out + ap.astype(jnp.float32) + am.astype(jnp.float32)
    return out.astype(jnp.bfloat16).reshape(rows, 1, -1)


def solution(mesh):
    fine = Mesh(mesh.devices.reshape(2, 4, 4, 8, 2), ("zh", "y", "x", "zl", "c"))
    frame, tensor = ("zh", "y", "x"), ("zl", "c")
    placed = (
        P(frame + tensor, None, None),
        P(),
        P(None, tensor),
        P(tensor, None),
        P(frame, None, tensor),
        P(frame, None, tensor),
        P(frame, None),
        P(),
    )
    return jax.shard_map(
        per_device,
        mesh=fine,
        in_specs=placed,
        out_specs=P(frame + tensor, None, None),
        check_vma=False,
    )
```

```python
import functools

import jax
import jax.numpy as jnp
from jax import lax
from jax.experimental import pallas as pl
from jax.experimental.pallas import tpu as pltpu
from jax.sharding import Mesh, PartitionSpec as P

HEAD_DIM = 128
EPSILON = 1e-06
MASKED = -1e30
RING = ("zh", "zl")
SWAP = [(0, 1), (1, 0)]
TURNS = (0, 1, 3, 2)
VMEM = pl.BlockSpec(memory_space=pltpu.VMEM)


def shift(step, size=16):
    return [(i, (i + step) % size) for i in range(size)]


def opposite(step):
    return [
        (2 * i + c, 2 * ((i + (step if c == 0 else -step)) % 16) + c)
        for i in range(16)
        for c in range(2)
    ]


def up(x):
    return lax.ppermute(x, RING, shift(1))


def down(x):
    return lax.ppermute(x, RING, shift(-1))


def prepare_kernel(tokens, gain, keys, values, pos, normed, payload):
    hidden = tokens[...].astype(jnp.float32)
    factor = lax.rsqrt(jnp.mean(hidden * hidden, axis=-1, keepdims=True) + EPSILON)
    normed[...] = (hidden * factor * gain[...]).astype(jnp.bfloat16)
    payload[0:48, :] = keys[...]
    payload[48:96, :] = values[...]
    high = lax.shift_right_logical(pos[...], 3)
    low = pos[...] - high * 8
    parts = [high[:, :256], high[:, 256:], low[:, :256], low[:, 256:]]
    parts = jnp.concatenate(parts + [jnp.zeros((12, 256), jnp.int32)], axis=0)
    payload[96:112, :] = parts.astype(jnp.float32).astype(jnp.bfloat16)


def attend_kernel(count, first, *refs):
    blocks = refs[:count]
    wq, wo, kv, bound, frame, out = (
        refs[count : count + 2],
        refs[count + 2 : count + 4],
        refs[count + 4 : count + 6],
        refs[count + 6],
        refs[count + 7],
        refs[count + 8],
    )
    rows = out.shape[0]
    x = jnp.concatenate([b[...] for b in blocks], axis=0)
    column = jnp.transpose(jnp.broadcast_to(bound[...].astype(jnp.float32), (8, 256)))
    column = column[first : first + rows, 0:1]
    bias = jnp.where(frame[...].astype(jnp.float32) <= column, 0.0, MASKED)
    groups = []
    for g in range(2):
        q = jnp.dot(x, wq[g][...], preferred_element_type=jnp.float32)
        q = (q * HEAD_DIM**-0.5).astype(jnp.bfloat16)
        heads = []
        for h in range(2):
            cols = slice(h * HEAD_DIM, (h + 1) * HEAD_DIM)
            s = [
                lax.dot_general(
                    q[:, cols],
                    kv[g][t, 0, :, cols],
                    (((1,), (1,)), ((), ())),
                    preferred_element_type=jnp.float32,
                )
                for t in range(4)
            ]
            s = jnp.concatenate(s, axis=1) + bias
            e = jnp.exp(s - jnp.max(s, axis=1, keepdims=True))
            total = jnp.sum(e, axis=1, keepdims=True)
            e = e.astype(jnp.bfloat16)
            a = sum(
                jnp.dot(
                    e[:, t * 384 : (t + 1) * 384],
                    kv[g][t, 1, :, cols],
                    preferred_element_type=jnp.float32,
                )
                for t in range(4)
            )
            heads.append((a / total).astype(jnp.bfloat16))
        groups.append(jnp.concatenate(heads, axis=1))
    for n in range(0, 4096, 1024):
        cols = slice(n, n + 1024)
        total = jnp.dot(groups[0], wo[0][:, cols], preferred_element_type=jnp.float32)
        total += jnp.dot(groups[1], wo[1][:, cols], preferred_element_type=jnp.float32)
        out[:, cols] = total.astype(jnp.bfloat16)


def attend(blocks, first, wq, wo, kv, bound, frame):
    count = len(blocks)
    rows = 32 * count
    return pl.pallas_call(
        functools.partial(attend_kernel, count, first),
        out_shape=jax.ShapeDtypeStruct((rows, 4096), jnp.bfloat16),
        in_specs=[VMEM] * (count + 8),
        out_specs=VMEM,
        compiler_params=pltpu.CompilerParams(vmem_limit_bytes=40 * 2**20),
        cost_estimate=pl.CostEstimate(
            flops=rows * 12 * 2**20, bytes_accessed=12 * 2**20, transcendentals=rows * 6144
        ),
        name="attend%d" % count,
    )(*blocks, *wq, *wo, *kv, bound, frame)


def per_device(tokens, gain, wq, wo, keys, values, token_pos, frame_pad):
    rows = tokens.shape[0]
    zh, y, x, zl, core = (lax.axis_index(a) for a in ("zh", "y", "x", "zl", "c"))
    z = zh * 8 + zl
    pos = token_pos.T
    own, mine = pl.pallas_call(
        prepare_kernel,
        out_shape=(
            jax.ShapeDtypeStruct((rows, 4096), jnp.bfloat16),
            jax.ShapeDtypeStruct((112, 256), jnp.bfloat16),
        ),
        in_specs=[VMEM] * 5,
        out_specs=(VMEM, VMEM),
        name="prepare",
    )(tokens.reshape(rows, 4096), gain.reshape(1, 4096), keys.reshape(48, 256), values.reshape(48, 256), pos)

    p1, m1 = up(own), down(own)
    p2, m2 = up(p1), down(m1)
    p3, m3 = up(p2), down(m2)
    far = lax.ppermute(jnp.where(core == 0, p3, m3), RING + ("c",), opposite(1))

    theirs = lax.ppermute(mine, "zh", SWAP)
    kv = jnp.stack([mine[:96].reshape(2, 48, 256), theirs[:96].reshape(2, 48, 256)], axis=1)
    kv = jnp.stack([kv] + [lax.ppermute(kv, "x", shift(s, 4)) for s in TURNS[1:]], axis=1)
    kv = kv.reshape(2, 384, 256)
    kv = jnp.stack([kv] + [lax.ppermute(kv, "y", shift(s, 4)) for s in TURNS[1:]])
    kv_other = lax.ppermute(kv, "c", SWAP)
    wq_other = lax.ppermute(wq, "c", SWAP)
    wo_other = lax.ppermute(wo, "c", SWAP)

    turns = jnp.array(TURNS, jnp.int32)
    ys, xs, halves = (y - turns) % 4, (x - turns) % 4, jnp.array([0, 1], jnp.int32) ^ zh
    place = halves[None, None, :] * 16 + ys[:, None, None] * 4 + xs[None, :, None]
    frame = (place[..., None] * 48 + jnp.arange(48, dtype=jnp.int32)).reshape(1, 1536)

    other = theirs[96:98].astype(jnp.int32) * 8 + theirs[98:100].astype(jnp.int32)
    other = other.reshape(1, 512)
    both = jnp.where(zh == 0, jnp.concatenate([pos, other]), jnp.concatenate([other, pos]))
    both = both.reshape(16, 2, rows)
    steps = (jnp.where(core == 0, -4, 4), -3, 3, -2, 2, -1, 1, 0)
    bound = jnp.concatenate(
        [lax.dynamic_slice(both, ((z + d) % 16, core, 0), (1, 1, rows)).reshape(1, rows) for d in steps],
        axis=1,
    )
    bound = jnp.minimum(bound, 1535 - frame_pad[0])

    given = ((wq, wq_other), (wo, wo_other), (kv, kv_other), bound, frame)
    part = attend([far, p3, m3], 0, *given)
    near = attend([p2, m2, p1, m1, own], 96, *given)
    wide = lambda v: v.astype(jnp.float32)
    thin = lambda v: v.astype(jnp.bfloat16)
    back = wide(lax.ppermute(part[:32], RING + ("c",), opposite(-1)))
    zero = jnp.zeros_like(back)
    ap = down(thin(wide(part[32:64]) + jnp.where(core == 0, back, zero)))
    am = up(thin(wide(part[64:96]) + jnp.where(core == 0, zero, back)))
    ap, am = down(thin(wide(near[:32]) + wide(ap))), up(thin(wide(near[32:64]) + wide(am)))
    ap, am = down(thin(wide(near[64:96]) + wide(ap))), up(thin(wide(near[96:128]) + wide(am)))
    out = wide(near[128:160]) + wide(ap) + wide(am)
    return thin(out).reshape(rows, 1, 4096)


def solution(mesh):
    fine = Mesh(mesh.devices.reshape(2, 4, 4, 8, 2), ("zh", "y", "x", "zl", "c"))
    frame, tensor = ("zh", "y", "x"), ("zl", "c")
    placed = (
        P(frame + tensor, None, None),
        P(),
        P(None, tensor),
        P(tensor, None),
        P(frame, None, tensor),
        P(frame, None, tensor),
        P(frame, None),
        P(),
    )
    return jax.shard_map(
        per_device,
        mesh=fine,
        in_specs=placed,
        out_specs=P(frame + tensor, None, None),
        check_vma=False,
    )
```

```python
import functools

import jax
import jax.numpy as jnp
from jax import lax
from jax.experimental import pallas as pl
from jax.experimental.pallas import tpu as pltpu
from jax.sharding import Mesh, PartitionSpec as P

HEAD_DIM = 128
EPSILON = 1e-06
MASKED = -1e30
RING = ("zh", "zl")
SWAP = [(0, 1), (1, 0)]
VMEM = pl.BlockSpec(memory_space=pltpu.VMEM)
HELD = pl.BlockSpec(memory_space=pl.ANY)


def opposite(step):
    return [
        (2 * i + c, 2 * ((i + (step if c == 0 else -step)) % 16) + c)
        for i in range(16)
        for c in range(2)
    ]


def along(x, step):
    return lax.ppermute(x, RING + ("c",), opposite(step))


def prepare_kernel(tokens, gain, keys, values, pos, normed, payload):
    hidden = tokens[...].astype(jnp.float32)
    factor = lax.rsqrt(jnp.mean(hidden * hidden, axis=-1, keepdims=True) + EPSILON)
    normed[...] = (hidden * factor * gain[...]).astype(jnp.bfloat16)
    payload[0:48, :] = keys[...]
    payload[48:96, :] = values[...]
    high = lax.shift_right_logical(pos[...], 3)
    low = pos[...] - high * 8
    parts = [high[:, :256], high[:, 256:], low[:, :256], low[:, 256:]]
    parts = jnp.concatenate(parts + [jnp.zeros((12, 256), jnp.int32)], axis=0)
    payload[96:112, :] = parts.astype(jnp.float32).astype(jnp.bfloat16)


def attend_kernel(count, first, *refs):
    blocks = refs[:count]
    sem = refs[-1]
    held = refs[count + 9 : count + 14]
    far = refs[count : count + 4] + (refs[count + 5],)
    copies = [pltpu.make_async_copy(far[i], held[i], sem.at[i]) for i in (0, 1, 4, 2, 3)]
    for copy in copies:
        copy.start()
    wq, wo, kv, bound, frame, out = (
        held[0:2],
        held[2:4],
        (refs[count + 4], held[4]),
        refs[count + 6],
        refs[count + 7],
        refs[count + 8],
    )
    rows = out.shape[0]
    x = jnp.concatenate([b[...] for b in blocks], axis=0)
    column = jnp.transpose(jnp.broadcast_to(bound[...].astype(jnp.float32), (8, 256)))
    column = column[first : first + rows, 0:1]
    bias = jnp.where(frame[...].astype(jnp.float32) <= column, 0.0, MASKED)
    groups = []
    for g in range(2):
        copies[g].wait()
        if g == 1:
            copies[2].wait()
        q = jnp.dot(x, wq[g][...], preferred_element_type=jnp.float32)
        q = (q * HEAD_DIM**-0.5).astype(jnp.bfloat16)
        heads = []
        for h in range(2):
            cols = slice(h * HEAD_DIM, (h + 1) * HEAD_DIM)
            s = [
                lax.dot_general(
                    q[:, cols],
                    kv[g][4 * t : 4 * t + 4, 0, :, :, cols].reshape(384, HEAD_DIM),
                    (((1,), (1,)), ((), ())),
                    preferred_element_type=jnp.float32,
                )
                for t in range(4)
            ]
            s = jnp.concatenate(s, axis=1) + bias
            e = jnp.exp(s - jnp.max(s, axis=1, keepdims=True))
            total = jnp.sum(e, axis=1, keepdims=True)
            e = e.astype(jnp.bfloat16)
            a = sum(
                jnp.dot(
                    e[:, t * 384 : (t + 1) * 384],
                    kv[g][4 * t : 4 * t + 4, 1, :, :, cols].reshape(384, HEAD_DIM),
                    preferred_element_type=jnp.float32,
                )
                for t in range(4)
            )
            heads.append((a / total).astype(jnp.bfloat16))
        groups.append(jnp.concatenate(heads, axis=1))
    copies[3].wait()
    copies[4].wait()
    for n in range(0, 4096, 1024):
        cols = slice(n, n + 1024)
        total = jnp.dot(groups[0], wo[0][:, cols], preferred_element_type=jnp.float32)
        total += jnp.dot(groups[1], wo[1][:, cols], preferred_element_type=jnp.float32)
        out[:, cols] = total.astype(jnp.bfloat16)


def attend(blocks, first, wq, wo, kv, bound, frame):
    count = len(blocks)
    rows = 32 * count
    return pl.pallas_call(
        functools.partial(attend_kernel, count, first),
        out_shape=jax.ShapeDtypeStruct((rows, 4096), jnp.bfloat16),
        in_specs=[VMEM] * count + [HELD] * 4 + [VMEM, HELD, VMEM, VMEM],
        out_specs=VMEM,
        scratch_shapes=[
            pltpu.VMEM((4096, 256), jnp.bfloat16),
            pltpu.VMEM((4096, 256), jnp.bfloat16),
            pltpu.VMEM((256, 4096), jnp.bfloat16),
            pltpu.VMEM((256, 4096), jnp.bfloat16),
            pltpu.VMEM((16, 2, 2, 48, 256), jnp.bfloat16),
            pltpu.SemaphoreType.DMA((5,)),
        ],
        compiler_params=pltpu.CompilerParams(vmem_limit_bytes=40 * 2**20),
        cost_estimate=pl.CostEstimate(
            flops=rows * 12 * 2**20, bytes_accessed=12 * 2**20, transcendentals=rows * 6144
        ),
        name="attend%d" % count,
    )(*blocks, *wq, *wo, *kv, bound, frame)


def per_device(tokens, gain, wq, wo, keys, values, token_pos, frame_pad):
    rows = tokens.shape[0]
    zh, zl, core = (lax.axis_index(a) for a in ("zh", "zl", "c"))
    z = zh * 8 + zl
    pos = token_pos.T
    own, mine = pl.pallas_call(
        prepare_kernel,
        out_shape=(
            jax.ShapeDtypeStruct((rows, 4096), jnp.bfloat16),
            jax.ShapeDtypeStruct((112, 256), jnp.bfloat16),
        ),
        in_specs=[VMEM] * 5,
        out_specs=(VMEM, VMEM),
        name="prepare",
    )(tokens.reshape(rows, 4096), gain.reshape(1, 4096), keys.reshape(48, 256), values.reshape(48, 256), pos)

    a1, b1 = along(own, 1), along(own, -1)

    theirs = lax.ppermute(mine, "zh", SWAP)
    kv = jnp.stack([mine[:96].reshape(2, 48, 256), theirs[:96].reshape(2, 48, 256)], axis=1)
    kv, a1, b1 = lax.optimization_barrier((kv, a1, b1))
    kv = jnp.broadcast_to(kv[None], (16, 2, 2, 48, 256))
    kv = lax.all_to_all(kv, ("y", "x"), 0, 0, tiled=True)
    a2, b2 = along(a1, 1), along(b1, -1)
    a3, b3 = along(a2, 1), along(b2, -1)
    kv, a3, b3 = lax.optimization_barrier((kv, a3, b3))
    a4 = along(a3, 1)
    kv_other = lax.ppermute(kv, "c", SWAP)
    wq_other = lax.ppermute(wq, "c", SWAP)
    wo_other = lax.ppermute(wo, "c", SWAP)

    halves = jnp.array([0, 1], jnp.int32) ^ zh
    place = halves[None, :] * 16 + jnp.arange(16, dtype=jnp.int32)[:, None]
    frame = (place[..., None] * 48 + jnp.arange(48, dtype=jnp.int32)).reshape(1, 1536)

    other = theirs[96:98].astype(jnp.int32) * 8 + theirs[98:100].astype(jnp.int32)
    other = other.reshape(1, 512)
    both = jnp.where(zh == 0, jnp.concatenate([pos, other]), jnp.concatenate([other, pos]))
    both = both.reshape(16, 2, rows)
    sign = 2 * core - 1
    steps = [sign * d for d in (4, 3, -3, 2, -2, 1, -1, 0)]
    bound = jnp.concatenate(
        [lax.dynamic_slice(both, ((z + d) % 16, core, 0), (1, 1, rows)).reshape(1, rows) for d in steps],
        axis=1,
    )
    bound = jnp.minimum(bound, 1535 - frame_pad[0])

    given = ((wq, wq_other), (wo, wo_other), (kv, kv_other), bound, frame)
    pair = attend([a3, b3], 32, *given)
    last = attend([a4], 0, *given)
    near = attend([a2, b2, a1, b1, own], 96, *given)
    wide = lambda v: v.astype(jnp.float32)
    thin = lambda v: v.astype(jnp.bfloat16)
    plus = lambda u, v: thin(wide(u) + wide(v))
    ap, bp = along(last, -1), along(pair[32:64], 1)
    ap, bp, near = lax.optimization_barrier((ap, bp, near))
    ap, bp = along(plus(pair[:32], ap), -1), along(plus(near[32:64], bp), 1)
    ap, bp = lax.optimization_barrier((ap, bp))
    ap, bp = along(plus(near[:32], ap), -1), along(plus(near[96:128], bp), 1)
    ap, bp = lax.optimization_barrier((ap, bp))
    ap = along(plus(near[64:96], ap), -1)
    out = wide(near[128:160]) + wide(ap) + wide(bp)
    return thin(out).reshape(rows, 1, 4096)


def solution(mesh):
    fine = Mesh(mesh.devices.reshape(2, 4, 4, 8, 2), ("zh", "y", "x", "zl", "c"))
    frame, tensor = ("zh", "y", "x"), ("zl", "c")
    placed = (
        P(frame + tensor, None, None),
        P(),
        P(None, tensor),
        P(tensor, None),
        P(frame, None, tensor),
        P(frame, None, tensor),
        P(frame, None),
        P(),
    )
    return jax.shard_map(
        per_device,
        mesh=fine,
        in_specs=placed,
        out_specs=P(frame + tensor, None, None),
        check_vma=False,
    )
```

```python
import functools

import jax
import jax.numpy as jnp
from jax import lax
from jax.experimental import pallas as pl
from jax.experimental.pallas import tpu as pltpu
from jax.sharding import Mesh, PartitionSpec as P

HEAD_DIM = 128
EPSILON = 1e-06
MASKED = -1e30
LIMIT = 48
STEPS = (4, 3, -3, 2, -2, 1, -1, 0)
RING = ("zh", "zl")
SWAP = [(0, 1), (1, 0)]
VMEM = pl.BlockSpec(memory_space=pltpu.VMEM)
HELD = pl.BlockSpec(memory_space=pltpu.HBM)


def opposite(step):
    return [
        (2 * i + c, 2 * ((i + (step if c == 0 else -step)) % 16) + c)
        for i in range(16)
        for c in range(2)
    ]


def along(x, step):
    return lax.ppermute(x, RING + ("c",), opposite(step))


def prepare_kernel(tokens, gain, keys, values, pos, normed, payload):
    hidden = tokens[...].astype(jnp.float32)
    factor = lax.rsqrt(jnp.mean(hidden * hidden, axis=-1, keepdims=True) + EPSILON)
    normed[...] = (hidden * factor * gain[...]).astype(jnp.bfloat16)
    payload[0:48, :] = keys[...]
    payload[48:96, :] = values[...]
    place = jnp.concatenate([pos[:, 32 * i : 32 * i + 32] for i in range(16)], axis=0)
    high = lax.shift_right_logical(place, 3)
    low = place - high * 8
    gap = jnp.zeros((16, 96), jnp.int32)
    parts = jnp.concatenate([high, gap, low, gap], axis=1)
    payload[96:112, :] = parts.astype(jnp.float32).astype(jnp.bfloat16)


def pack_kernel(frame_pad, mine, theirs, spread, bound):
    for i in range(16):
        for part in range(2):
            for half, source in enumerate((mine, theirs)):
                spread[i, part, half] = source[48 * part : 48 * part + 48, :]
    zh, zl, core = (lax.axis_index(a) for a in ("zh", "zl", "c"))
    places = []
    for source in (mine, theirs):
        parts = source[96:112, :].astype(jnp.float32)
        places.append(parts[:, 0:32] * 8.0 + parts[:, 128:160])
    row = lax.broadcasted_iota(jnp.int32, (16, 32), 0)
    found = []
    for step in STEPS:
        z = (zh * 8 + zl + step * (2 * core - 1) + 16) % 16
        place = jnp.where(z // 8 == zh, places[0], places[1])
        place = jnp.where(row == z % 8 * 2 + core, place, 0.0)
        found.append(jnp.sum(place, axis=0, keepdims=True))
    last = (1535 - frame_pad[0]).astype(jnp.float32)
    bound[...] = jnp.minimum(jnp.concatenate(found, axis=1), last)


def attend_kernel(count, first, *refs):
    blocks, outs = refs[:count], refs[count + 7 : 2 * count + 7]
    held, sem = refs[2 * count + 7 : 2 * count + 11], refs[-1]
    copies = [pltpu.make_async_copy(refs[count + i], held[i], sem.at[i]) for i in range(4)]
    for copy in copies:
        copy.start()
    wq, wo, kv = held[:2], held[2:], refs[count + 4 : count + 6]
    bound = refs[count + 6]
    rows = 32 * count
    x = jnp.concatenate([b[...] for b in blocks], axis=0)
    column = jnp.transpose(jnp.broadcast_to(bound[...], (8, 256)))
    column = column[first : first + rows, 0:1]
    zh = lax.axis_index("zh")
    index = lax.broadcasted_iota(jnp.int32, (1, 1536), 1)
    shard = lax.shift_right_logical(index * 1366, 16)
    half = (shard & 1) ^ zh
    frame = half * 768 + lax.shift_right_logical(shard, 1) * 48 + (index - shard * 48)
    bias = jnp.where(frame.astype(jnp.float32) <= column, 0.0, MASKED)
    groups = []
    for g in range(2):
        copies[g].wait()
        q = jnp.dot(x, wq[g][...], preferred_element_type=jnp.float32)
        q = (q * HEAD_DIM**-0.5).astype(jnp.bfloat16)
        heads = []
        for h in range(2):
            cols = slice(h * HEAD_DIM, (h + 1) * HEAD_DIM)
            s = [
                lax.dot_general(
                    q[:, cols],
                    kv[g][4 * t : 4 * t + 4, 0, :, :, cols].reshape(384, HEAD_DIM),
                    (((1,), (1,)), ((), ())),
                    preferred_element_type=jnp.float32,
                )
                for t in range(4)
            ]
            s = jnp.concatenate(s, axis=1) + bias
            e = jnp.exp(s - jnp.max(s, axis=1, keepdims=True))
            total = jnp.sum(e, axis=1, keepdims=True)
            e = e.astype(jnp.bfloat16)
            a = sum(
                jnp.dot(
                    e[:, t * 384 : (t + 1) * 384],
                    kv[g][4 * t : 4 * t + 4, 1, :, :, cols].reshape(384, HEAD_DIM),
                    preferred_element_type=jnp.float32,
                )
                for t in range(4)
            )
            heads.append((a / total).astype(jnp.bfloat16))
        groups.append(jnp.concatenate(heads, axis=1))
    copies[2].wait()
    copies[3].wait()
    for n in range(0, 4096, 1024):
        cols = slice(n, n + 1024)
        total = jnp.dot(groups[0], wo[0][:, cols], preferred_element_type=jnp.float32)
        total += jnp.dot(groups[1], wo[1][:, cols], preferred_element_type=jnp.float32)
        total = total.astype(jnp.bfloat16)
        for i in range(count):
            outs[i][:, cols] = total[32 * i : 32 * i + 32, :]


def attend(blocks, first, wq, wo, kv, bound):
    count = len(blocks)
    rows = 32 * count
    return pl.pallas_call(
        functools.partial(attend_kernel, count, first),
        out_shape=[jax.ShapeDtypeStruct((32, 4096), jnp.bfloat16)] * count,
        in_specs=[VMEM] * count + [HELD] * 4 + [VMEM] * 3,
        out_specs=[VMEM] * count,
        scratch_shapes=[pltpu.VMEM((4096, 256), jnp.bfloat16)] * 2
        + [pltpu.VMEM((256, 4096), jnp.bfloat16)] * 2
        + [pltpu.SemaphoreType.DMA((4,))],
        compiler_params=pltpu.CompilerParams(vmem_limit_bytes=LIMIT * 2**20),
        cost_estimate=pl.CostEstimate(
            flops=rows * 12 * 2**20, bytes_accessed=12 * 2**20, transcendentals=rows * 6144
        ),
        name="attend%d" % count,
    )(*blocks, *wq, *wo, *kv, bound)


def per_device(tokens, gain, wq, wo, keys, values, token_pos, frame_pad):
    rows = tokens.shape[0]
    pos = token_pos.T
    own, mine = pl.pallas_call(
        prepare_kernel,
        out_shape=(
            jax.ShapeDtypeStruct((rows, 4096), jnp.bfloat16),
            jax.ShapeDtypeStruct((112, 256), jnp.bfloat16),
        ),
        in_specs=[VMEM] * 5,
        out_specs=(VMEM, VMEM),
        name="prepare",
    )(tokens.reshape(rows, 4096), gain.reshape(1, 4096), keys.reshape(48, 256), values.reshape(48, 256), pos)

    a1, b1 = along(own, 1), along(own, -1)

    theirs = lax.ppermute(mine, "zh", SWAP)
    theirs, a1, b1 = lax.optimization_barrier((theirs, a1, b1))
    wq_other = lax.ppermute(wq, "c", SWAP)
    wo_other = lax.ppermute(wo, "c", SWAP)
    kv, bound = pl.pallas_call(
        pack_kernel,
        out_shape=(
            jax.ShapeDtypeStruct((16, 2, 2, 48, 256), jnp.bfloat16),
            jax.ShapeDtypeStruct((1, 256), jnp.float32),
        ),
        in_specs=[pl.BlockSpec(memory_space=pltpu.SMEM), VMEM, VMEM],
        out_specs=(VMEM, VMEM),
        compiler_params=pltpu.CompilerParams(vmem_limit_bytes=8 * 2**20),
        name="pack",
    )(frame_pad, mine, theirs)
    kv = lax.all_to_all(kv, ("y", "x"), 0, 0, tiled=True)
    a2, b2 = along(a1, 1), along(b1, -1)
    a3, b3 = along(a2, 1), along(b2, -1)
    a4 = along(a2, 2)
    kv, a3, a4, b3 = lax.optimization_barrier((kv, a3, a4, b3))
    kv_other = lax.ppermute(kv, "c", SWAP)

    given = ((wq, wq_other), (wo, wo_other), (kv, kv_other), bound)
    far = attend([a4, a3, b3], 0, *given)
    near = attend([a2, b2, a1, b1, own], 96, *given)
    wide = lambda v: v.astype(jnp.float32)
    thin = lambda v: v.astype(jnp.bfloat16)
    plus = lambda u, v: thin(wide(u) + wide(v))
    ap, bp, mid = along(far[1], -1), along(far[2], 1), along(far[0], -2)
    ap, bp, mid, near = lax.optimization_barrier((ap, bp, mid, near))
    ap, bp = along(thin(wide(near[0]) + wide(ap) + wide(mid)), -1), along(plus(near[1], bp), 1)
    ap, bp = lax.optimization_barrier((ap, bp))
    ap, bp = along(plus(near[2], ap), -1), along(plus(near[3], bp), 1)
    out = wide(near[4]) + wide(ap) + wide(bp)
    return thin(out).reshape(rows, 1, 4096)


def solution(mesh):
    fine = Mesh(mesh.devices.reshape(2, 4, 4, 8, 2), ("zh", "y", "x", "zl", "c"))
    frame, tensor = ("zh", "y", "x"), ("zl", "c")
    placed = (
        P(frame + tensor, None, None),
        P(),
        P(None, tensor),
        P(tensor, None),
        P(frame, None, tensor),
        P(frame, None, tensor),
        P(frame, None),
        P(),
    )
    return jax.shard_map(
        per_device,
        mesh=fine,
        in_specs=placed,
        out_specs=P(frame + tensor, None, None),
        check_vma=False,
    )
```

```python
import functools

import jax
import jax.numpy as jnp
from jax import lax
from jax.experimental import pallas as pl
from jax.experimental.pallas import tpu as pltpu
from jax.sharding import Mesh, PartitionSpec as P

HEAD_DIM = 128
EPSILON = 1e-06
MASKED = -1e30
LIMIT = 48
STEPS = (4, 3, -3, 2, -2, 1, -1, 0)
RING = ("zh", "zl")
SWAP = [(0, 1), (1, 0)]
VMEM = pl.BlockSpec(memory_space=pltpu.VMEM)
HELD = pl.BlockSpec(memory_space=pltpu.HBM)


def opposite(step):
    return [
        (2 * i + c, 2 * ((i + (step if c == 0 else -step)) % 16) + c)
        for i in range(16)
        for c in range(2)
    ]


def along(x, step):
    return lax.ppermute(x, RING + ("c",), opposite(step))


def prepare_kernel(tokens, gain, keys, values, pos, normed, payload):
    hidden = tokens[...].astype(jnp.float32)
    factor = lax.rsqrt(jnp.mean(hidden * hidden, axis=-1, keepdims=True) + EPSILON)
    normed[...] = (hidden * factor * gain[...]).astype(jnp.bfloat16)
    payload[0:48, :] = keys[...]
    payload[48:96, :] = values[...]
    place = jnp.concatenate([pos[:, 32 * i : 32 * i + 32] for i in range(16)], axis=0)
    high = lax.shift_right_logical(place, 3)
    low = place - high * 8
    gap = jnp.zeros((16, 96), jnp.int32)
    parts = jnp.concatenate([high, gap, low, gap], axis=1)
    payload[96:112, :] = parts.astype(jnp.float32).astype(jnp.bfloat16)


def pack_kernel(frame_pad, mine, theirs, spread, bound):
    for i in range(16):
        for part in range(2):
            for half, source in enumerate((mine, theirs)):
                spread[i, part, half] = source[48 * part : 48 * part + 48, :]
    zh, zl, core = (lax.axis_index(a) for a in ("zh", "zl", "c"))
    places = []
    for source in (mine, theirs):
        parts = source[96:112, :].astype(jnp.float32)
        places.append(parts[:, 0:32] * 8.0 + parts[:, 128:160])
    row = lax.broadcasted_iota(jnp.int32, (16, 32), 0)
    found = []
    for step in STEPS:
        z = (zh * 8 + zl + step * (2 * core - 1) + 16) % 16
        place = jnp.where(z // 8 == zh, places[0], places[1])
        place = jnp.where(row == z % 8 * 2 + core, place, 0.0)
        found.append(jnp.sum(place, axis=0, keepdims=True))
    last = (1535 - frame_pad[0]).astype(jnp.float32)
    bound[...] = jnp.minimum(jnp.concatenate(found, axis=1), last)


def attended(x, wq, kv, bias):
    q = jnp.dot(x, wq[...], preferred_element_type=jnp.float32)
    q = (q * HEAD_DIM**-0.5).astype(jnp.bfloat16)
    heads = []
    for h in range(2):
        cols = slice(h * HEAD_DIM, (h + 1) * HEAD_DIM)
        s = [
            lax.dot_general(
                q[:, cols],
                kv[4 * t : 4 * t + 4, 0, :, :, cols].reshape(384, HEAD_DIM),
                (((1,), (1,)), ((), ())),
                preferred_element_type=jnp.float32,
            )
            for t in range(4)
        ]
        s = jnp.concatenate(s, axis=1) + bias
        e = jnp.exp(s - jnp.max(s, axis=1, keepdims=True))
        total = jnp.sum(e, axis=1, keepdims=True)
        e = e.astype(jnp.bfloat16)
        a = sum(
            jnp.dot(
                e[:, t * 384 : (t + 1) * 384],
                kv[4 * t : 4 * t + 4, 1, :, :, cols].reshape(384, HEAD_DIM),
                preferred_element_type=jnp.float32,
            )
            for t in range(4)
        )
        heads.append((a / total).astype(jnp.bfloat16))
    return jnp.concatenate(heads, axis=1)


def shade(bound, first, rows):
    column = jnp.transpose(jnp.broadcast_to(bound[...], (8, 256)))
    column = column[first : first + rows, 0:1]
    zh = lax.axis_index("zh")
    index = lax.broadcasted_iota(jnp.int32, (1, 1536), 1)
    shard = lax.shift_right_logical(index * 1366, 16)
    half = (shard & 1) ^ zh
    frame = half * 768 + lax.shift_right_logical(shard, 1) * 48 + (index - shard * 48)
    return jnp.where(frame.astype(jnp.float32) <= column, 0.0, MASKED)


def fetch(sources, held, sem):
    copies = [pltpu.make_async_copy(u, v, sem.at[i]) for i, (u, v) in enumerate(zip(sources, held))]
    for copy in copies:
        copy.start()
    return copies


def project(groups, wo, outs):
    for n in range(0, 4096, 1024):
        cols = slice(n, n + 1024)
        total = jnp.dot(groups[0], wo[0][:, cols], preferred_element_type=jnp.float32)
        total += jnp.dot(groups[1], wo[1][:, cols], preferred_element_type=jnp.float32)
        total = total.astype(jnp.bfloat16)
        for i, out in enumerate(outs):
            out[:, cols] = total[32 * i : 32 * i + 32, :]


def attend_kernel(count, first, *refs):
    blocks, outs = refs[:count], refs[count + 7 : 2 * count + 7]
    held = refs[2 * count + 7 : 2 * count + 11]
    copies = fetch(refs[count : count + 4], held, refs[-1])
    x = jnp.concatenate([b[...] for b in blocks], axis=0)
    bias = shade(refs[count + 6], first, 32 * count)
    groups = []
    for g in range(2):
        copies[g].wait()
        groups.append(attended(x, held[g], refs[count + 4 + g], bias))
    copies[2].wait()
    copies[3].wait()
    project(groups, held[2:], outs)


def begin_kernel(count, first, *refs):
    blocks = refs[:count]
    wq, kv, bound, out, held, sem = refs[count:]
    (copy,) = fetch((wq,), (held,), sem)
    x = jnp.concatenate([b[...] for b in blocks], axis=0)
    bias = shade(bound, first, 32 * count)
    copy.wait()
    out[...] = attended(x, held, kv, bias)


def finish_kernel(count, first, *refs):
    blocks, outs = refs[:count], refs[count + 6 : 2 * count + 6]
    kv, bound, done = refs[count + 3 : count + 6]
    held = refs[2 * count + 6 : 2 * count + 9]
    copies = fetch(refs[count : count + 3], held, refs[-1])
    x = jnp.concatenate([b[...] for b in blocks], axis=0)
    bias = shade(bound, first, 32 * count)
    copies[0].wait()
    groups = (done[...], attended(x, held[0], kv, bias))
    copies[1].wait()
    copies[2].wait()
    project(groups, held[1:], outs)


def begin(blocks, first, wq, kv, bound):
    count = len(blocks)
    rows = 32 * count
    return pl.pallas_call(
        functools.partial(begin_kernel, count, first),
        out_shape=jax.ShapeDtypeStruct((rows, 256), jnp.bfloat16),
        in_specs=[VMEM] * count + [HELD, VMEM, VMEM],
        out_specs=VMEM,
        scratch_shapes=[pltpu.VMEM((4096, 256), jnp.bfloat16), pltpu.SemaphoreType.DMA((1,))],
        compiler_params=pltpu.CompilerParams(vmem_limit_bytes=50 * 2**20),
        cost_estimate=pl.CostEstimate(
            flops=rows * 4 * 2**20, bytes_accessed=4 * 2**20, transcendentals=rows * 3072
        ),
        name="begin%d" % count,
    )(*blocks, wq, kv, bound)


def finish(blocks, first, wq, wo, kv, bound, done):
    count = len(blocks)
    rows = 32 * count
    return pl.pallas_call(
        functools.partial(finish_kernel, count, first),
        out_shape=[jax.ShapeDtypeStruct((32, 4096), jnp.bfloat16)] * count,
        in_specs=[VMEM] * count + [HELD] * 3 + [VMEM] * 3,
        out_specs=[VMEM] * count,
        scratch_shapes=[pltpu.VMEM((4096, 256), jnp.bfloat16)]
        + [pltpu.VMEM((256, 4096), jnp.bfloat16)] * 2
        + [pltpu.SemaphoreType.DMA((3,))],
        compiler_params=pltpu.CompilerParams(vmem_limit_bytes=LIMIT * 2**20),
        cost_estimate=pl.CostEstimate(
            flops=rows * 8 * 2**20, bytes_accessed=8 * 2**20, transcendentals=rows * 3072
        ),
        name="finish%d" % count,
    )(*blocks, wq, *wo, kv, bound, done)


def attend(blocks, first, wq, wo, kv, bound):
    count = len(blocks)
    rows = 32 * count
    return pl.pallas_call(
        functools.partial(attend_kernel, count, first),
        out_shape=[jax.ShapeDtypeStruct((32, 4096), jnp.bfloat16)] * count,
        in_specs=[VMEM] * count + [HELD] * 4 + [VMEM] * 3,
        out_specs=[VMEM] * count,
        scratch_shapes=[pltpu.VMEM((4096, 256), jnp.bfloat16)] * 2
        + [pltpu.VMEM((256, 4096), jnp.bfloat16)] * 2
        + [pltpu.SemaphoreType.DMA((4,))],
        compiler_params=pltpu.CompilerParams(vmem_limit_bytes=LIMIT * 2**20),
        cost_estimate=pl.CostEstimate(
            flops=rows * 12 * 2**20, bytes_accessed=12 * 2**20, transcendentals=rows * 6144
        ),
        name="attend%d" % count,
    )(*blocks, *wq, *wo, *kv, bound)


def per_device(tokens, gain, wq, wo, keys, values, token_pos, frame_pad):
    rows = tokens.shape[0]
    pos = token_pos.T
    own, mine = pl.pallas_call(
        prepare_kernel,
        out_shape=(
            jax.ShapeDtypeStruct((rows, 4096), jnp.bfloat16),
            jax.ShapeDtypeStruct((112, 256), jnp.bfloat16),
        ),
        in_specs=[VMEM] * 5,
        out_specs=(VMEM, VMEM),
        name="prepare",
    )(tokens.reshape(rows, 4096), gain.reshape(1, 4096), keys.reshape(48, 256), values.reshape(48, 256), pos)

    a1, b1 = along(own, 1), along(own, -1)

    theirs = lax.ppermute(mine, "zh", SWAP)
    theirs, a1, b1 = lax.optimization_barrier((theirs, a1, b1))
    wq_other = lax.ppermute(wq, "c", SWAP)
    wo_other = lax.ppermute(wo, "c", SWAP)
    kv, bound = pl.pallas_call(
        pack_kernel,
        out_shape=(
            jax.ShapeDtypeStruct((16, 2, 2, 48, 256), jnp.bfloat16),
            jax.ShapeDtypeStruct((1, 256), jnp.float32),
        ),
        in_specs=[pl.BlockSpec(memory_space=pltpu.SMEM), VMEM, VMEM],
        out_specs=(VMEM, VMEM),
        compiler_params=pltpu.CompilerParams(vmem_limit_bytes=8 * 2**20),
        name="pack",
    )(frame_pad, mine, theirs)
    kv = lax.all_to_all(kv, ("y", "x"), 0, 0, tiled=True)
    a2, b2 = along(a1, 1), along(b1, -1)
    a3, b3 = along(a2, 1), along(b2, -1)
    a4 = along(a2, 2)
    kv, a3, a4, b3 = lax.optimization_barrier((kv, a3, a4, b3))
    kv_other = lax.ppermute(kv, "c", SWAP)

    given = ((wq, wq_other), (wo, wo_other), (kv, kv_other), bound)
    half = begin([a4, a3, b3], 0, wq, kv, bound)
    far = finish([a4, a3, b3], 0, wq_other, (wo, wo_other), kv_other, bound, half)
    near = attend([a2, b2, a1, b1, own], 96, *given)
    wide = lambda v: v.astype(jnp.float32)
    thin = lambda v: v.astype(jnp.bfloat16)
    plus = lambda u, v: thin(wide(u) + wide(v))
    ap, bp, mid = along(far[1], -1), along(far[2], 1), along(far[0], -2)
    ap, bp, mid, near = lax.optimization_barrier((ap, bp, mid, near))
    ap, bp = along(thin(wide(near[0]) + wide(ap) + wide(mid)), -1), along(plus(near[1], bp), 1)
    ap, bp = lax.optimization_barrier((ap, bp))
    ap, bp = along(plus(near[2], ap), -1), along(plus(near[3], bp), 1)
    out = wide(near[4]) + wide(ap) + wide(bp)
    return thin(out).reshape(rows, 1, 4096)


def solution(mesh):
    fine = Mesh(mesh.devices.reshape(2, 4, 4, 8, 2), ("zh", "y", "x", "zl", "c"))
    frame, tensor = ("zh", "y", "x"), ("zl", "c")
    placed = (
        P(frame + tensor, None, None),
        P(),
        P(None, tensor),
        P(tensor, None),
        P(frame, None, tensor),
        P(frame, None, tensor),
        P(frame, None),
        P(),
    )
    return jax.shard_map(
        per_device,
        mesh=fine,
        in_specs=placed,
        out_specs=P(frame + tensor, None, None),
        check_vma=False,
    )
```

```python
import functools

import jax
import jax.numpy as jnp
from jax import lax
from jax.experimental import pallas as pl
from jax.experimental.pallas import tpu as pltpu
from jax.sharding import Mesh, PartitionSpec as P

HEAD_DIM = 128
EPSILON = 1e-06
MASKED = -1e30
LIMIT = 48
STEPS = (4, 3, -3, 2, -2, 1, -1, 0)
RING = ("zh", "zl")
SWAP = [(0, 1), (1, 0)]
VMEM = pl.BlockSpec(memory_space=pltpu.VMEM)
HELD = pl.BlockSpec(memory_space=pltpu.HBM)


def opposite(step):
    return [
        (2 * i + c, 2 * ((i + (step if c == 0 else -step)) % 16) + c)
        for i in range(16)
        for c in range(2)
    ]


def along(x, step):
    return lax.ppermute(x, RING + ("c",), opposite(step))


def prepare_kernel(tokens, gain, keys, values, pos, normed, payload):
    hidden = tokens[...].astype(jnp.float32)
    factor = lax.rsqrt(jnp.mean(hidden * hidden, axis=-1, keepdims=True) + EPSILON)
    normed[...] = (hidden * factor * gain[...]).astype(jnp.bfloat16)
    payload[0:48, :] = keys[...]
    payload[48:96, :] = values[...]
    place = jnp.concatenate([pos[:, 32 * i : 32 * i + 32] for i in range(16)], axis=0)
    high = lax.shift_right_logical(place, 3)
    low = place - high * 8
    gap = jnp.zeros((16, 96), jnp.int32)
    parts = jnp.concatenate([high, gap, low, gap], axis=1)
    payload[96:112, :] = parts.astype(jnp.float32).astype(jnp.bfloat16)


def pack_kernel(frame_pad, mine, theirs, spread, bound):
    for i in range(16):
        for part in range(2):
            for half, source in enumerate((mine, theirs)):
                spread[i, part, half] = source[48 * part : 48 * part + 48, :]
    zh, zl, core = (lax.axis_index(a) for a in ("zh", "zl", "c"))
    places = []
    for source in (mine, theirs):
        parts = source[96:112, :].astype(jnp.float32)
        places.append(parts[:, 0:32] * 8.0 + parts[:, 128:160])
    row = lax.broadcasted_iota(jnp.int32, (16, 32), 0)
    found = []
    for step in STEPS:
        z = (zh * 8 + zl + step * (2 * core - 1) + 16) % 16
        place = jnp.where(z // 8 == zh, places[0], places[1])
        place = jnp.where(row == z % 8 * 2 + core, place, 0.0)
        found.append(jnp.sum(place, axis=0, keepdims=True))
    last = (1535 - frame_pad[0]).astype(jnp.float32)
    bound[...] = jnp.minimum(jnp.concatenate(found, axis=1), last)


def attended(x, wq, kv, bias):
    q = jnp.dot(x, wq[...], preferred_element_type=jnp.float32)
    q = (q * HEAD_DIM**-0.5).astype(jnp.bfloat16)
    heads = []
    for h in range(2):
        cols = slice(h * HEAD_DIM, (h + 1) * HEAD_DIM)
        s = [
            lax.dot_general(
                q[:, cols],
                kv[4 * t : 4 * t + 4, 0, :, :, cols].reshape(384, HEAD_DIM),
                (((1,), (1,)), ((), ())),
                preferred_element_type=jnp.float32,
            )
            for t in range(4)
        ]
        s = jnp.concatenate(s, axis=1) + bias
        e = jnp.exp(s - jnp.max(s, axis=1, keepdims=True))
        total = jnp.sum(e, axis=1, keepdims=True)
        e = e.astype(jnp.bfloat16)
        a = sum(
            jnp.dot(
                e[:, t * 384 : (t + 1) * 384],
                kv[4 * t : 4 * t + 4, 1, :, :, cols].reshape(384, HEAD_DIM),
                preferred_element_type=jnp.float32,
            )
            for t in range(4)
        )
        heads.append((a / total).astype(jnp.bfloat16))
    return jnp.concatenate(heads, axis=1)


def shade(bound, first, rows):
    column = jnp.transpose(jnp.broadcast_to(bound[...], (8, 256)))
    column = column[first : first + rows, 0:1]
    zh = lax.axis_index("zh")
    index = lax.broadcasted_iota(jnp.int32, (1, 1536), 1)
    shard = lax.shift_right_logical(index * 1366, 16)
    half = (shard & 1) ^ zh
    frame = half * 768 + lax.shift_right_logical(shard, 1) * 48 + (index - shard * 48)
    return jnp.where(frame.astype(jnp.float32) <= column, 0.0, MASKED)


def fetch(sources, held, sem):
    copies = [pltpu.make_async_copy(u, v, sem.at[i]) for i, (u, v) in enumerate(zip(sources, held))]
    for copy in copies:
        copy.start()
    return copies


def project(groups, wo, outs):
    for n in range(0, 4096, 1024):
        cols = slice(n, n + 1024)
        total = jnp.dot(groups[0], wo[0][:, cols], preferred_element_type=jnp.float32)
        total += jnp.dot(groups[1], wo[1][:, cols], preferred_element_type=jnp.float32)
        total = total.astype(jnp.bfloat16)
        for i, out in enumerate(outs):
            out[:, cols] = total[32 * i : 32 * i + 32, :]


def attend_kernel(count, first, *refs):
    blocks, outs = refs[:count], refs[count + 7 : 2 * count + 7]
    held = refs[2 * count + 7 : 2 * count + 11]
    copies = fetch(refs[count : count + 4], held, refs[-1])
    x = jnp.concatenate([b[...] for b in blocks], axis=0)
    bias = shade(refs[count + 6], first, 32 * count)
    groups = []
    for g in range(2):
        copies[g].wait()
        groups.append(attended(x, held[g], refs[count + 4 + g], bias))
    copies[2].wait()
    copies[3].wait()
    project(groups, held[2:], outs)


def begin_kernel(count, first, *refs):
    blocks = refs[:count]
    wq, kv, bound, out, held, sem = refs[count:]
    (copy,) = fetch((wq,), (held,), sem)
    x = jnp.concatenate([b[...] for b in blocks], axis=0)
    bias = shade(bound, first, 32 * count)
    copy.wait()
    out[...] = attended(x, held, kv, bias)


def finish_kernel(count, first, *refs):
    blocks, outs = refs[:count], refs[count + 6 : 2 * count + 6]
    kv, bound, done = refs[count + 3 : count + 6]
    held = refs[2 * count + 6 : 2 * count + 9]
    copies = fetch(refs[count : count + 3], held, refs[-1])
    x = jnp.concatenate([b[...] for b in blocks], axis=0)
    bias = shade(bound, first, 32 * count)
    copies[0].wait()
    groups = (done[...], attended(x, held[0], kv, bias))
    copies[1].wait()
    copies[2].wait()
    project(groups, held[1:], outs)


def begin(blocks, first, wq, kv, bound):
    count = len(blocks)
    rows = 32 * count
    return pl.pallas_call(
        functools.partial(begin_kernel, count, first),
        out_shape=jax.ShapeDtypeStruct((rows, 256), jnp.bfloat16),
        in_specs=[VMEM] * count + [HELD, VMEM, VMEM],
        out_specs=VMEM,
        scratch_shapes=[pltpu.VMEM((4096, 256), jnp.bfloat16), pltpu.SemaphoreType.DMA((1,))],
        compiler_params=pltpu.CompilerParams(vmem_limit_bytes=50 * 2**20),
        cost_estimate=pl.CostEstimate(
            flops=rows * 4 * 2**20, bytes_accessed=4 * 2**20, transcendentals=rows * 3072
        ),
        name="begin%d" % count,
    )(*blocks, wq, kv, bound)


def finish(blocks, first, wq, wo, kv, bound, done):
    count = len(blocks)
    rows = 32 * count
    return pl.pallas_call(
        functools.partial(finish_kernel, count, first),
        out_shape=[jax.ShapeDtypeStruct((32, 4096), jnp.bfloat16)] * count,
        in_specs=[VMEM] * count + [HELD] * 3 + [VMEM] * 3,
        out_specs=[VMEM] * count,
        scratch_shapes=[pltpu.VMEM((4096, 256), jnp.bfloat16)]
        + [pltpu.VMEM((256, 4096), jnp.bfloat16)] * 2
        + [pltpu.SemaphoreType.DMA((3,))],
        compiler_params=pltpu.CompilerParams(vmem_limit_bytes=LIMIT * 2**20),
        cost_estimate=pl.CostEstimate(
            flops=rows * 8 * 2**20, bytes_accessed=8 * 2**20, transcendentals=rows * 3072
        ),
        name="finish%d" % count,
    )(*blocks, wq, *wo, kv, bound, done)


def attend(blocks, first, wq, wo, kv, bound):
    count = len(blocks)
    rows = 32 * count
    return pl.pallas_call(
        functools.partial(attend_kernel, count, first),
        out_shape=[jax.ShapeDtypeStruct((32, 4096), jnp.bfloat16)] * count,
        in_specs=[VMEM] * count + [HELD] * 4 + [VMEM] * 3,
        out_specs=[VMEM] * count,
        scratch_shapes=[pltpu.VMEM((4096, 256), jnp.bfloat16)] * 2
        + [pltpu.VMEM((256, 4096), jnp.bfloat16)] * 2
        + [pltpu.SemaphoreType.DMA((4,))],
        compiler_params=pltpu.CompilerParams(vmem_limit_bytes=LIMIT * 2**20),
        cost_estimate=pl.CostEstimate(
            flops=rows * 12 * 2**20, bytes_accessed=12 * 2**20, transcendentals=rows * 6144
        ),
        name="attend%d" % count,
    )(*blocks, *wq, *wo, *kv, bound)


def per_device(tokens, gain, wq, wo, keys, values, token_pos, frame_pad):
    rows = tokens.shape[0]
    pos = token_pos.T
    own, mine = pl.pallas_call(
        prepare_kernel,
        out_shape=(
            jax.ShapeDtypeStruct((rows, 4096), jnp.bfloat16),
            jax.ShapeDtypeStruct((112, 256), jnp.bfloat16),
        ),
        in_specs=[VMEM] * 5,
        out_specs=(VMEM, VMEM),
        name="prepare",
    )(tokens.reshape(rows, 4096), gain.reshape(1, 4096), keys.reshape(48, 256), values.reshape(48, 256), pos)

    b1, a1 = along(own, -1), along(own, 1)

    theirs = lax.ppermute(mine, "zh", SWAP)
    theirs, b1, a1 = lax.optimization_barrier((theirs, b1, a1))
    wq_other = lax.ppermute(wq, "c", SWAP)
    wo_other = lax.ppermute(wo, "c", SWAP)
    kv, bound = pl.pallas_call(
        pack_kernel,
        out_shape=(
            jax.ShapeDtypeStruct((16, 2, 2, 48, 256), jnp.bfloat16),
            jax.ShapeDtypeStruct((1, 256), jnp.float32),
        ),
        in_specs=[pl.BlockSpec(memory_space=pltpu.SMEM), VMEM, VMEM],
        out_specs=(VMEM, VMEM),
        compiler_params=pltpu.CompilerParams(vmem_limit_bytes=8 * 2**20),
        name="pack",
    )(frame_pad, mine, theirs)
    kv = lax.all_to_all(kv, ("y", "x"), 0, 0, tiled=True)
    a2, b2 = along(a1, 1), along(b1, -1)
    a3, b3 = along(a2, 1), along(b2, -1)
    a4 = along(a2, 2)
    kv, a4, a3, b3 = lax.optimization_barrier((kv, a4, a3, b3))
    kv_other = lax.ppermute(kv, "c", SWAP)

    given = ((wq, wq_other), (wo, wo_other), (kv, kv_other), bound)
    half = begin([a4, a3, b3], 0, wq, kv, bound)
    far = finish([a4, a3, b3], 0, wq_other, (wo, wo_other), kv_other, bound, half)
    near = attend([a2, b2, a1, b1, own], 96, *given)
    wide = lambda v: v.astype(jnp.float32)
    thin = lambda v: v.astype(jnp.bfloat16)
    plus = lambda u, v: thin(wide(u) + wide(v))
    mid, ap, bp = along(far[0], -2), along(far[1], -1), along(far[2], 1)
    mid, ap, bp, near = lax.optimization_barrier((mid, ap, bp, near))
    ap, bp = along(thin(wide(near[0]) + wide(ap) + wide(mid)), -1), along(plus(near[1], bp), 1)
    ap, bp = lax.optimization_barrier((ap, bp))
    ap, bp = along(plus(near[2], ap), -1), along(plus(near[3], bp), 1)
    out = wide(near[4]) + wide(ap) + wide(bp)
    return thin(out).reshape(rows, 1, 4096)


def solution(mesh):
    fine = Mesh(mesh.devices.reshape(2, 4, 4, 8, 2), ("zh", "y", "x", "zl", "c"))
    frame, tensor = ("zh", "y", "x"), ("zl", "c")
    placed = (
        P(frame + tensor, None, None),
        P(),
        P(None, tensor),
        P(tensor, None),
        P(frame, None, tensor),
        P(frame, None, tensor),
        P(frame, None),
        P(),
    )
    return jax.shard_map(
        per_device,
        mesh=fine,
        in_specs=placed,
        out_specs=P(frame + tensor, None, None),
        check_vma=False,
    )
```

```python
import functools

import jax
import jax.numpy as jnp
from jax import lax
from jax.experimental import pallas as pl
from jax.experimental.pallas import tpu as pltpu
from jax.sharding import Mesh, PartitionSpec as P

HEAD_DIM = 128
EPSILON = 1e-06
MASKED = -1e30
LIMIT = 48
STEPS = (4, 3, -3, 2, -2, 1, -1, 0)
RING = ("zh", "zl")
SWAP = [(0, 1), (1, 0)]
VMEM = pl.BlockSpec(memory_space=pltpu.VMEM)
HELD = pl.BlockSpec(memory_space=pltpu.HBM)


def opposite(step):
    return [
        (2 * i + c, 2 * ((i + (step if c == 0 else -step)) % 16) + c)
        for i in range(16)
        for c in range(2)
    ]


def along(x, step):
    return lax.ppermute(x, RING + ("c",), opposite(step))


def prepare_kernel(tokens, gain, keys, values, pos, normed, payload):
    hidden = tokens[...].astype(jnp.float32)
    factor = lax.rsqrt(jnp.mean(hidden * hidden, axis=-1, keepdims=True) + EPSILON)
    normed[...] = (hidden * factor * gain[...]).astype(jnp.bfloat16)
    payload[0:48, :] = keys[...]
    payload[48:96, :] = values[...]
    place = jnp.concatenate([pos[:, 32 * i : 32 * i + 32] for i in range(16)], axis=0)
    high = lax.shift_right_logical(place, 3)
    low = place - high * 8
    gap = jnp.zeros((16, 96), jnp.int32)
    parts = jnp.concatenate([high, gap, low, gap], axis=1)
    payload[96:112, :] = parts.astype(jnp.float32).astype(jnp.bfloat16)


def pack_kernel(frame_pad, mine, theirs, spread, bound):
    for i in range(16):
        for part in range(2):
            for half, source in enumerate((mine, theirs)):
                spread[i, part, half] = source[48 * part : 48 * part + 48, :]
    zh, zl, core = (lax.axis_index(a) for a in ("zh", "zl", "c"))
    places = []
    for source in (mine, theirs):
        parts = source[96:112, :].astype(jnp.float32)
        places.append(parts[:, 0:32] * 8.0 + parts[:, 128:160])
    row = lax.broadcasted_iota(jnp.int32, (16, 32), 0)
    found = []
    for step in STEPS:
        z = (zh * 8 + zl + step * (2 * core - 1) + 16) % 16
        place = jnp.where(z // 8 == zh, places[0], places[1])
        place = jnp.where(row == z % 8 * 2 + core, place, 0.0)
        found.append(jnp.sum(place, axis=0, keepdims=True))
    last = (1535 - frame_pad[0]).astype(jnp.float32)
    bound[...] = jnp.minimum(jnp.concatenate(found, axis=1), last)


def attend_kernel(count, first, *refs):
    blocks, outs = refs[:count], refs[count + 7 : 2 * count + 7]
    held, sem = refs[2 * count + 7 : 2 * count + 11], refs[-1]
    copies = [pltpu.make_async_copy(refs[count + i], held[i], sem.at[i]) for i in range(4)]
    for copy in copies:
        copy.start()
    wq, wo, kv = held[:2], held[2:], refs[count + 4 : count + 6]
    bound = refs[count + 6]
    rows = 32 * count
    x = jnp.concatenate([b[...] for b in blocks], axis=0)
    column = jnp.transpose(jnp.broadcast_to(bound[...], (8, 256)))
    column = column[first : first + rows, 0:1]
    zh = lax.axis_index("zh")
    index = lax.broadcasted_iota(jnp.int32, (1, 1536), 1)
    shard = lax.shift_right_logical(index * 1366, 16)
    half = (shard & 1) ^ zh
    frame = half * 768 + lax.shift_right_logical(shard, 1) * 48 + (index - shard * 48)
    bias = jnp.where(frame.astype(jnp.float32) <= column, 0.0, MASKED)
    groups = []
    for g in range(2):
        copies[g].wait()
        q = jnp.dot(x, wq[g][...], preferred_element_type=jnp.float32)
        q = (q * HEAD_DIM**-0.5).astype(jnp.bfloat16)
        heads = []
        for h in range(2):
            cols = slice(h * HEAD_DIM, (h + 1) * HEAD_DIM)
            s = [
                lax.dot_general(
                    q[:, cols],
                    kv[g][4 * t : 4 * t + 4, 0, :, :, cols].reshape(384, HEAD_DIM),
                    (((1,), (1,)), ((), ())),
                    preferred_element_type=jnp.float32,
                )
                for t in range(4)
            ]
            s = jnp.concatenate(s, axis=1) + bias
            e = jnp.exp(s - jnp.max(s, axis=1, keepdims=True))
            total = jnp.sum(e, axis=1, keepdims=True)
            e = e.astype(jnp.bfloat16)
            a = sum(
                jnp.dot(
                    e[:, t * 384 : (t + 1) * 384],
                    kv[g][4 * t : 4 * t + 4, 1, :, :, cols].reshape(384, HEAD_DIM),
                    preferred_element_type=jnp.float32,
                )
                for t in range(4)
            )
            heads.append((a / total).astype(jnp.bfloat16))
        groups.append(jnp.concatenate(heads, axis=1))
    copies[2].wait()
    copies[3].wait()
    for n in range(0, 4096, 1024):
        cols = slice(n, n + 1024)
        total = jnp.dot(groups[0], wo[0][:, cols], preferred_element_type=jnp.float32)
        total += jnp.dot(groups[1], wo[1][:, cols], preferred_element_type=jnp.float32)
        total = total.astype(jnp.bfloat16)
        for i in range(count):
            outs[i][:, cols] = total[32 * i : 32 * i + 32, :]


def attend(blocks, first, wq, wo, kv, bound):
    count = len(blocks)
    rows = 32 * count
    return pl.pallas_call(
        functools.partial(attend_kernel, count, first),
        out_shape=[jax.ShapeDtypeStruct((32, 4096), jnp.bfloat16)] * count,
        in_specs=[VMEM] * count + [HELD] * 4 + [VMEM] * 3,
        out_specs=[VMEM] * count,
        scratch_shapes=[pltpu.VMEM((4096, 256), jnp.bfloat16)] * 2
        + [pltpu.VMEM((256, 4096), jnp.bfloat16)] * 2
        + [pltpu.SemaphoreType.DMA((4,))],
        compiler_params=pltpu.CompilerParams(vmem_limit_bytes=LIMIT * 2**20),
        cost_estimate=pl.CostEstimate(
            flops=rows * 12 * 2**20, bytes_accessed=12 * 2**20, transcendentals=rows * 6144
        ),
        name="attend%d" % count,
    )(*blocks, *wq, *wo, *kv, bound)


def per_device(tokens, gain, wq, wo, keys, values, token_pos, frame_pad):
    rows = tokens.shape[0]
    pos = token_pos.T
    own, mine = pl.pallas_call(
        prepare_kernel,
        out_shape=(
            jax.ShapeDtypeStruct((rows, 4096), jnp.bfloat16),
            jax.ShapeDtypeStruct((112, 256), jnp.bfloat16),
        ),
        in_specs=[VMEM] * 5,
        out_specs=(VMEM, VMEM),
        name="prepare",
    )(tokens.reshape(rows, 4096), gain.reshape(1, 4096), keys.reshape(48, 256), values.reshape(48, 256), pos)

    a1, b1 = along(own, 1), along(own, -1)

    theirs = lax.ppermute(mine, "zh", SWAP)
    theirs, a1, b1 = lax.optimization_barrier((theirs, a1, b1))
    wq_other = lax.ppermute(wq, "c", SWAP)
    wo_other = lax.ppermute(wo, "c", SWAP)
    kv, bound = pl.pallas_call(
        pack_kernel,
        out_shape=(
            jax.ShapeDtypeStruct((16, 2, 2, 48, 256), jnp.bfloat16),
            jax.ShapeDtypeStruct((1, 256), jnp.float32),
        ),
        in_specs=[pl.BlockSpec(memory_space=pltpu.SMEM), VMEM, VMEM],
        out_specs=(VMEM, VMEM),
        compiler_params=pltpu.CompilerParams(vmem_limit_bytes=8 * 2**20),
        name="pack",
    )(frame_pad, mine, theirs)
    kv = lax.all_to_all(kv, ("y", "x"), 0, 0, tiled=True)
    a2, b2 = along(a1, 1), along(b1, -1)
    a3, b3 = along(a2, 1), along(b2, -1)
    a4 = along(a2, 2)
    kv, a3, a4, b3 = lax.optimization_barrier((kv, a3, a4, b3))
    kv_other = lax.ppermute(kv, "c", SWAP)

    given = ((wq, wq_other), (wo, wo_other), (kv, kv_other), bound)
    far = attend([a4, a3, b3], 0, *given)
    near = attend([a2, b2, a1, b1, own], 96, *given)
    wide = lambda v: v.astype(jnp.float32)
    thin = lambda v: v.astype(jnp.bfloat16)
    plus = lambda u, v: thin(wide(u) + wide(v))
    mid, ap, bp = along(far[0], -2), along(far[1], -1), along(far[2], 1)
    mid, ap, bp, near = lax.optimization_barrier((mid, ap, bp, near))
    ap, bp = along(thin(wide(near[0]) + wide(ap) + wide(mid)), -1), along(plus(near[1], bp), 1)
    ap, bp = lax.optimization_barrier((ap, bp))
    ap, bp = along(plus(near[2], ap), -1), along(plus(near[3], bp), 1)
    out = wide(near[4]) + wide(ap) + wide(bp)
    return thin(out).reshape(rows, 1, 4096)


def solution(mesh):
    fine = Mesh(mesh.devices.reshape(2, 4, 4, 8, 2), ("zh", "y", "x", "zl", "c"))
    frame, tensor = ("zh", "y", "x"), ("zl", "c")
    placed = (
        P(frame + tensor, None, None),
        P(),
        P(None, tensor),
        P(tensor, None),
        P(frame, None, tensor),
        P(frame, None, tensor),
        P(frame, None),
        P(),
    )
    return jax.shard_map(
        per_device,
        mesh=fine,
        in_specs=placed,
        out_specs=P(frame + tensor, None, None),
        check_vma=False,
    )
```

```python
import functools

import jax
import jax.numpy as jnp
from jax import lax
from jax.experimental import pallas as pl
from jax.experimental.pallas import tpu as pltpu
from jax.sharding import Mesh, PartitionSpec as P

HEAD_DIM = 128
EPSILON = 1e-06
MASKED = -1e30
LIMIT = 48
STEPS = (4, 3, -3, 2, -2, 1, -1, 0)
RING = ("zh", "zl")
SWAP = [(0, 1), (1, 0)]
VMEM = pl.BlockSpec(memory_space=pltpu.VMEM)
HELD = pl.BlockSpec(memory_space=pltpu.HBM)


def opposite(step):
    return [
        (2 * i + c, 2 * ((i + (step if c == 0 else -step)) % 16) + c)
        for i in range(16)
        for c in range(2)
    ]


def along(x, step):
    return lax.ppermute(x, RING + ("c",), opposite(step))


def prepare_kernel(tokens, gain, keys, values, pos, normed, payload):
    hidden = tokens[...].astype(jnp.float32)
    factor = lax.rsqrt(jnp.mean(hidden * hidden, axis=-1, keepdims=True) + EPSILON)
    normed[...] = (hidden * factor * gain[...]).astype(jnp.bfloat16)
    payload[0:48, :] = keys[...]
    payload[48:96, :] = values[...]
    place = jnp.concatenate([pos[:, 32 * i : 32 * i + 32] for i in range(16)], axis=0)
    high = lax.shift_right_logical(place, 3)
    low = place - high * 8
    gap = jnp.zeros((16, 96), jnp.int32)
    parts = jnp.concatenate([high, gap, low, gap], axis=1)
    payload[96:112, :] = parts.astype(jnp.float32).astype(jnp.bfloat16)


def pack_kernel(frame_pad, mine, theirs, spread, bound):
    for i in range(16):
        for part in range(2):
            for half, source in enumerate((mine, theirs)):
                spread[i, part, half] = source[48 * part : 48 * part + 48, :]
    zh, zl, core = (lax.axis_index(a) for a in ("zh", "zl", "c"))
    places = []
    for source in (mine, theirs):
        parts = source[96:112, :].astype(jnp.float32)
        places.append(parts[:, 0:32] * 8.0 + parts[:, 128:160])
    row = lax.broadcasted_iota(jnp.int32, (16, 32), 0)
    found = []
    for step in STEPS:
        z = (zh * 8 + zl + step * (2 * core - 1) + 16) % 16
        place = jnp.where(z // 8 == zh, places[0], places[1])
        place = jnp.where(row == z % 8 * 2 + core, place, 0.0)
        found.append(jnp.sum(place, axis=0, keepdims=True))
    last = (1535 - frame_pad[0]).astype(jnp.float32)
    bound[...] = jnp.minimum(jnp.concatenate(found, axis=1), last)


def attend_kernel(count, first, *refs):
    blocks, outs = refs[:count], refs[count + 7 : 2 * count + 7]
    held, sem = refs[2 * count + 7 : 2 * count + 11], refs[-1]
    copies = [pltpu.make_async_copy(refs[count + i], held[i], sem.at[i]) for i in range(4)]
    for copy in copies:
        copy.start()
    wq, wo, kv = held[:2], held[2:], refs[count + 4 : count + 6]
    bound = refs[count + 6]
    rows = 32 * count
    x = jnp.concatenate([b[...] for b in blocks], axis=0)
    column = jnp.transpose(jnp.broadcast_to(bound[...], (8, 256)))
    column = column[first : first + rows, 0:1]
    zh = lax.axis_index("zh")
    index = lax.broadcasted_iota(jnp.int32, (1, 1536), 1)
    shard = lax.shift_right_logical(index * 1366, 16)
    half = (shard & 1) ^ zh
    frame = half * 768 + lax.shift_right_logical(shard, 1) * 48 + (index - shard * 48)
    bias = jnp.where(frame.astype(jnp.float32) <= column, 0.0, MASKED)
    groups = []
    for g in range(2):
        copies[g].wait()
        q = jnp.dot(x, wq[g][...], preferred_element_type=jnp.float32)
        q = (q * HEAD_DIM**-0.5).astype(jnp.bfloat16)
        heads = []
        for h in range(2):
            cols = slice(h * HEAD_DIM, (h + 1) * HEAD_DIM)
            s = [
                lax.dot_general(
                    q[:, cols],
                    kv[g][4 * t : 4 * t + 4, 0, :, :, cols].reshape(384, HEAD_DIM),
                    (((1,), (1,)), ((), ())),
                    preferred_element_type=jnp.float32,
                )
                for t in range(4)
            ]
            s = jnp.concatenate(s, axis=1) + bias
            e = jnp.exp(s - jnp.max(s, axis=1, keepdims=True))
            total = jnp.sum(e, axis=1, keepdims=True)
            e = e.astype(jnp.bfloat16)
            a = sum(
                jnp.dot(
                    e[:, t * 384 : (t + 1) * 384],
                    kv[g][4 * t : 4 * t + 4, 1, :, :, cols].reshape(384, HEAD_DIM),
                    preferred_element_type=jnp.float32,
                )
                for t in range(4)
            )
            heads.append((a / total).astype(jnp.bfloat16))
        groups.append(jnp.concatenate(heads, axis=1))
    copies[2].wait()
    copies[3].wait()
    for n in range(0, 4096, 1024):
        cols = slice(n, n + 1024)
        total = jnp.dot(groups[0], wo[0][:, cols], preferred_element_type=jnp.float32)
        total += jnp.dot(groups[1], wo[1][:, cols], preferred_element_type=jnp.float32)
        total = total.astype(jnp.bfloat16)
        for i in range(count):
            outs[i][:, cols] = total[32 * i : 32 * i + 32, :]


def attend(blocks, first, wq, wo, kv, bound):
    count = len(blocks)
    rows = 32 * count
    return pl.pallas_call(
        functools.partial(attend_kernel, count, first),
        out_shape=[jax.ShapeDtypeStruct((32, 4096), jnp.bfloat16)] * count,
        in_specs=[VMEM] * count + [HELD] * 4 + [VMEM] * 3,
        out_specs=[VMEM] * count,
        scratch_shapes=[pltpu.VMEM((4096, 256), jnp.bfloat16)] * 2
        + [pltpu.VMEM((256, 4096), jnp.bfloat16)] * 2
        + [pltpu.SemaphoreType.DMA((4,))],
        compiler_params=pltpu.CompilerParams(vmem_limit_bytes=LIMIT * 2**20),
        cost_estimate=pl.CostEstimate(
            flops=rows * 12 * 2**20, bytes_accessed=12 * 2**20, transcendentals=rows * 6144
        ),
        name="attend%d" % count,
    )(*blocks, *wq, *wo, *kv, bound)


def per_device(tokens, gain, wq, wo, keys, values, token_pos, frame_pad):
    rows = tokens.shape[0]
    pos = token_pos.T
    own, mine = pl.pallas_call(
        prepare_kernel,
        out_shape=(
            jax.ShapeDtypeStruct((rows, 4096), jnp.bfloat16),
            jax.ShapeDtypeStruct((112, 256), jnp.bfloat16),
        ),
        in_specs=[VMEM] * 5,
        out_specs=(VMEM, VMEM),
        name="prepare",
    )(tokens.reshape(rows, 4096), gain.reshape(1, 4096), keys.reshape(48, 256), values.reshape(48, 256), pos)

    a1, b1 = along(own, 1), along(own, -1)

    theirs = lax.ppermute(mine, "zh", SWAP)
    theirs, a1, b1 = lax.optimization_barrier((theirs, a1, b1))
    wq_other = lax.ppermute(wq, "c", SWAP)
    wo_other = lax.ppermute(wo, "c", SWAP)
    kv, bound = pl.pallas_call(
        pack_kernel,
        out_shape=(
            jax.ShapeDtypeStruct((16, 2, 2, 48, 256), jnp.bfloat16),
            jax.ShapeDtypeStruct((1, 256), jnp.float32),
        ),
        in_specs=[pl.BlockSpec(memory_space=pltpu.SMEM), VMEM, VMEM],
        out_specs=(VMEM, VMEM),
        compiler_params=pltpu.CompilerParams(vmem_limit_bytes=8 * 2**20),
        name="pack",
    )(frame_pad, mine, theirs)
    kv = lax.all_to_all(kv, ("y", "x"), 0, 0, tiled=True)
    a2, b2 = along(a1, 1), along(b1, -1)
    a3, b3 = along(a2, 1), along(b2, -1)
    a4 = along(a2, 2)
    kv, a3, a4, b3 = lax.optimization_barrier((kv, a3, a4, b3))
    kv_other = lax.ppermute(kv, "c", SWAP)

    given = ((wq, wq_other), (wo, wo_other), (kv, kv_other), bound)
    far = attend([a4, a3, b3], 0, *given)
    near = attend([a2, b2, a1, b1, own], 96, *given)
    wide = lambda v: v.astype(jnp.float32)
    thin = lambda v: v.astype(jnp.bfloat16)
    plus = lambda u, v: thin(wide(u) + wide(v))
    mid, ap, bp = along(far[0], -2), along(far[1], -1), along(far[2], 1)
    mid, ap, bp, near = lax.optimization_barrier((mid, ap, bp, near))
    ap, bp = along(thin(wide(near[0]) + wide(ap) + wide(mid)), -1), along(plus(near[1], bp), 1)
    ap, bp = along(plus(near[2], ap), -1), along(plus(near[3], bp), 1)
    out = wide(near[4]) + wide(ap) + wide(bp)
    return thin(out).reshape(rows, 1, 4096)


def solution(mesh):
    fine = Mesh(mesh.devices.reshape(2, 4, 4, 8, 2), ("zh", "y", "x", "zl", "c"))
    frame, tensor = ("zh", "y", "x"), ("zl", "c")
    placed = (
        P(frame + tensor, None, None),
        P(),
        P(None, tensor),
        P(tensor, None),
        P(frame, None, tensor),
        P(frame, None, tensor),
        P(frame, None),
        P(),
    )
    return jax.shard_map(
        per_device,
        mesh=fine,
        in_specs=placed,
        out_specs=P(frame + tensor, None, None),
        check_vma=False,
    )
```
